128 devices in a mesh: member: 4 (over z), space: 32 (over y, x, core).
Axes of the slice: x: 4, y: 4, z: 4, core: 2. Of those that a mesh axis runs over, the one named last changes fastest.
Arguments:
- particles: float32 [32, 2, 800, 800], P('member', None, 'space'), may hold values from -8 to 8
- loglik_grad: float32 [32, 2, 800, 800], P('member', None, 'space'), may hold values from -9.1552734e-05 to 9.1552734e-05
- wave_prev: float32 [32, 2, 800, 800], P('member', None, 'space'), may hold values from -6 to 6
- wave_now: float32 [32, 2, 800, 800], P('member', None, 'space'), may hold values from -6 to 6
- ghosts: float32 [32, 8, 800, 800], P('member', None, 'space'), may hold values from -6 to 6
- src_cell: int32 [32], P('member'), may hold values from 0 to 639999
Outputs:
- new_particles: float32 [32, 2, 800, 800], P('member', None, 'space')
- wave_before: float32 [32, 2, 800, 800], P('member', None, 'space')
- wave_after: float32 [32, 2, 800, 800], P('member', None, 'space')
The draws below stay inside these ranges and needn't reach their ends.
Inputs may be any that keep to these rules, and one draw needn't show every extreme that they name: `src_cell`: the flat index 800 * x + y of each particle's source cell on depth plane 0.
All inputs are finite; a program needn't handle non-finite values.
Results may differ from the reference program's by a relative error of at most 0.0003.
Values sent between devices are 32-bit elements; how exact they have to be, the bound alone decides.
A program may use at most 128 MiB of HBM per device.

```python
import math
import jax
import jax.numpy as jnp
from jax import lax

CX = 25
NY = 800
NZ = 2
GHOST = 4
STEPS = 4
PARTICLES = 32
NX = 800


def draw_particles(key, part):
    base_key = jax.random.fold_in(key, 11)
    scale_key, block_key, value_key = jax.random.split(base_key, 3)
    shape = (PARTICLES, NZ, NX, NY)
    blocks = NX // CX
    scales = jnp.exp(jax.random.uniform(scale_key, (PARTICLES, 1, 1, 1), jnp.float32, math.log(0.5), math.log(2.0)))
    block_scales = jnp.exp(jax.random.uniform(block_key, (PARTICLES, 1, blocks, 1), jnp.float32, -0.7, 0.7))
    spread = scales * jnp.repeat(block_scales, CX, axis=2)
    values = jnp.clip(jax.random.normal(value_key, shape, jnp.float32), -4.0, 4.0)
    result = spread * values
    return jnp.clip(result, -8.0, 8.0)


def plant(entries, rng, smallest, top_value):
    dims = entries.shape
    place = [jax.random.randint(jax.random.fold_in(rng, axis), (), 0, dims[axis]) for axis in range(len(dims))]
    entries = entries.at[tuple(place)].set(smallest)
    longest = dims.index(max(dims))
    place[longest] = (place[longest] + 1) % dims[longest]
    return entries.at[tuple(place)].set(top_value)


def block_scale(own_key, shape, cuts, smallest, top_value):
    def one(position, blocks):
        heights = jax.random.uniform(jax.random.fold_in(jax.random.fold_in(own_key, 6), position), (blocks,), jnp.float32, smallest / len(cuts), top_value / len(cuts))
        return jnp.repeat(jnp.exp(heights), shape[position] // blocks).reshape((-1,) + (1,) * (len(shape) - position - 1))

    loudness = one(*cuts[0])
    for cut in cuts[1:]:
        loudness = loudness * one(*cut)
    return loudness


def noise(rng, dims, scale, reach, cuts=(), held_as=jnp.bfloat16):
    array = scale * jax.random.normal(rng, dims, jnp.float32)
    if cuts:
        array = array * block_scale(rng, dims, cuts, -0.22, 0.18)
    return jnp.clip(array, -reach, reach).astype(held_as)


def setup_inputs(seed: int = 0) -> dict:
    splits = jax.random.split(jax.random.key(seed), 7)
    return {
        "particles": draw_particles(jax.random.fold_in(splits[6], 71), 0),
        "loglik_grad": noise(splits[1], (PARTICLES, NZ, NX, NY), (8.0 / (NX * NY * NZ)), 9.1552734375e-05, ((0, 4), (2, 32)), jnp.float32),
        "wave_prev": noise(splits[2], (PARTICLES, NZ, NX, NY), 1.0, 6.0, ((0, 4), (2, 32)), jnp.float32),
        "wave_now": noise(splits[3], (PARTICLES, NZ, NX, NY), 1.0, 6.0, ((0, 4), (2, 32)), jnp.float32),
        "ghosts": noise(splits[4], (PARTICLES, 2 * GHOST, NX, NY), 1.0, 6.0, ((0, 4), (2, 32)), jnp.float32),
        "src_cell": plant(jax.random.randint(splits[5], (PARTICLES,), 0, NX * NY), jax.random.fold_in(splits[5], 1), 0, (NX * NY) - 1).astype(jnp.int32),
    }


weights = (-205.0 / 72.0, 8.0 / 5.0, -1.0 / 5.0, 8.0 / 315.0, -1.0 / 560.0)
step_size = 0.25
courant = 0.3


def laplace(wide, top, bottom):
    extent = wide.shape[-2] - 8
    center = wide[..., 4:4 + extent, :]
    depth = center.shape[-3]
    across = center.shape[-1]
    pad_spec = [(0, 0)] * (center.ndim - 1) + [(4, 4)]
    ypad = jnp.pad(center, pad_spec)
    column = jnp.concatenate([top, center, bottom], axis=-3)
    total = (3.0 * weights[0]) * center
    for offset in range(1, 5):
        total = total + weights[offset] * (wide[..., 4 + offset:4 + offset + extent, :] + wide[..., 4 - offset:4 - offset + extent, :])
        total = total + weights[offset] * (ypad[..., 4 + offset:4 + offset + across] + ypad[..., 4 - offset:4 - offset + across])
        total = total + weights[offset] * (column[..., 4 + offset:4 + offset + depth, :, :] + column[..., 4 - offset:4 - offset + depth, :, :])
    return total


def reference(particles, loglik_grad, wave_prev, wave_now, ghosts, src_cell):
    count = particles.shape[0]
    flat = particles.reshape(count, -1)
    gflat = loglik_grad.reshape(count, -1)

    def one_row(single):
        return jnp.sum(jnp.square(flat - single[None, :]), axis=1)

    dist = lax.map(one_row, flat)
    offdiag = 1.0 - jnp.eye(count, dtype=jnp.float32)
    band = jnp.sum(dist * offdiag) / (count * (count - 1) * math.log(count + 1))
    kern = jnp.exp(-dist / band)
    kernel_grad = jnp.dot(kern, gflat, precision=lax.Precision.HIGHEST, preferred_element_type=jnp.float32)
    kernel_pos = jnp.dot(kern, flat, precision=lax.Precision.HIGHEST, preferred_element_type=jnp.float32)
    moved = flat + step_size * ((0.5 * band) * kernel_grad + jnp.sum(kern, axis=1)[:, None] * flat - kernel_pos)
    new_particles = moved.reshape(particles.shape)

    coef = jnp.square(courant * (1.0 + 0.3 * jnp.tanh(particles)))

    def propagate(items):
        prev, now, ghost, factor, source = items
        src_x = source // NY
        src_y = source % NY
        xs = jnp.arange(NX, dtype=jnp.int32)
        ys = jnp.arange(NY, dtype=jnp.int32)
        spot = ((xs[:, None] == src_x) & (ys[None, :] == src_y)).astype(jnp.float32)
        plane = (jnp.arange(NZ, dtype=jnp.int32) == 0).astype(jnp.float32)
        inject = plane[:, None, None] * spot[None, :, :]
        top = ghost[:GHOST]
        bottom = ghost[GHOST:]
        for step in range(STEPS):
            wide = jnp.pad(now, ((0, 0), (4, 4), (0, 0)))
            amplitude = 2.0 * math.cos(1.3 * step)
            following = 2.0 * now - prev + factor * laplace(wide, top, bottom) + amplitude * inject
            prev, now = now, following
        return prev, now

    wave_before, wave_after = lax.map(propagate, (wave_prev, wave_now, ghosts, coef, src_cell))
    return new_particles, wave_before, wave_after
```

```python
import functools
import math

import jax
import jax.numpy as jnp
from jax import lax
from jax.experimental import pallas as pl
from jax.experimental.pallas import tpu as pltpu
from jax.sharding import PartitionSpec as P

MESH = pl.DeviceIdType.MESH
F32 = jnp.float32
GHOST = 4
STEPS = 4
MEMBERS = 4
OWN = 8
COUNT = 32
ROWS = 25
NY = 800
WIDE = 896
HALF = 384
TAIL = 768
CHUNKS = 5
CHUNK = ROWS // CHUNKS

weights = (-205.0 / 72.0, 8.0 / 5.0, -1.0 / 5.0, 8.0 / 315.0, -1.0 / 560.0)
step_size = 0.25
courant = 0.3


def tail_rows(half):
    return list(range(13)) if half == 0 else list(range(13, ROWS))


def kernel(
    x_hbm, g_hbm, wp_hbm, wn_hbm, gh_hbm, src_hbm,
    new, before, after,
    src_ref, xv, gv, prev, wave, gh, gz, coef,
    cells, tails, xtail, gtail, out, otail, ntail,
    spot, acc, part, kmat,
    load_sem, src_sem, own_sem, send_sem, recv_sem, hsend_sem, hrecv_sem, rsend_sem, rrecv_sem,
):
    me = lax.axis_index("member")
    sp = lax.axis_index("space")
    spaces = 32
    my_plane = me // 2
    my_lane = pl.multiple_of((me % 2) * HALF, 128)
    right = (sp + 1) % spaces
    left = (sp + spaces - 1) % spaces
    has_left = sp > 0
    has_right = sp < spaces - 1
    group = sp // 8
    place = sp % 8

    def loads(n, src, dst_of):
        return [
            pltpu.make_async_copy(src.at[p], dst_of(p), load_sem.at[n, p])
            for p in range(OWN)
        ]

    load_x = loads(0, x_hbm, lambda p: xv.at[:, :, p, :])
    load_n = loads(1, wn_hbm, lambda p: wave.at[0, pl.ds(GHOST, ROWS), :, p, :])
    load_h = loads(2, gh_hbm, lambda p: gh.at[:, :, p, :])
    load_p = loads(3, wp_hbm, lambda p: prev.at[:, :, p, :])
    load_g = loads(4, g_hbm, lambda p: gv.at[:, :, p, :])
    for group_of in (load_x, load_n, load_h, load_p, load_g):
        for c in group_of:
            c.start()

    load_src = pltpu.make_async_copy(src_hbm, src_ref, src_sem)
    load_src.start()

    barrier = pltpu.get_barrier_semaphore()
    for d in range(1, MEMBERS):
        pl.semaphore_signal(
            barrier, inc=1, device_id={"member": (me + d) % MEMBERS, "space": sp}, device_id_type=MESH
        )
    peers = [group * 8 + (place + d) % 8 for d in range(1, 8)]
    peers += [((group + d) % 4) * 8 + place for d in range(1, 4)]
    peers += [left, right]
    for peer in peers:
        pl.semaphore_signal(barrier, inc=1, device_id={"member": me, "space": peer}, device_id_type=MESH)

    acc[...] = jnp.zeros_like(acc)
    sub = lax.broadcasted_iota(jnp.int32, (OWN, NY), 0)
    lane = lax.broadcasted_iota(jnp.int32, (OWN, NY), 1)
    sx = jnp.full((OWN, NY), -1, jnp.int32)
    sy = jnp.full((OWN, NY), -1, jnp.int32)
    load_src.wait()
    for p in range(OWN):
        flat = src_ref[p]
        row = lax.div(flat, jnp.int32(NY))
        sx = jnp.where(sub == p, row - sp * ROWS, sx)
        sy = jnp.where(sub == p, flat - row * NY, sy)
    spot[...] = jnp.where(lane == sy, sx, -1)

    @pl.when(jnp.logical_not(has_left))
    def _():
        for t in range(STEPS):
            wave[t, 0:GHOST] = jnp.zeros((GHOST, 2, OWN, NY), F32)

    @pl.when(jnp.logical_not(has_right))
    def _():
        for t in range(STEPS):
            wave[t, GHOST + ROWS :] = jnp.zeros((GHOST, 2, OWN, NY), F32)

    pl.semaphore_wait(barrier, 15)

    def exchange(phase, k, d):
        c = (me + d) % MEMBERS
        source, tail = (xv, xtail) if phase == 0 else (gv, gtail)
        at = pl.ds(pl.multiple_of(phase * COUNT + me * OWN, 8), OWN)
        if k == CHUNKS:
            src = tail.at[c]
            dst = tails.at[:, at, :]
        else:
            rows = pl.ds(k * CHUNK, CHUNK)
            src = source.at[rows, c // 2, :, pl.ds(pl.multiple_of((c % 2) * HALF, 128), HALF)]
            dst = cells.at[rows, at, :]
        if d == 0:
            return pltpu.make_async_copy(src, dst, own_sem.at[phase, k])
        return pltpu.make_async_remote_copy(
            src_ref=src,
            dst_ref=dst,
            send_sem=send_sem.at[phase, k, c],
            recv_sem=recv_sem.at[phase, k, me],
            device_id={"member": c, "space": sp},
            device_id_type=MESH,
        )

    def arrived(phase, k):
        for d in range(1, MEMBERS):
            c = (me + d) % MEMBERS
            at = pl.ds(pl.multiple_of(phase * COUNT + c * OWN, 8), OWN)
            if k == CHUNKS:
                dst = tails.at[:, at, :]
            else:
                dst = cells.at[pl.ds(k * CHUNK, CHUNK), at, :]
            pltpu.make_async_remote_copy(
                src_ref=dst,
                dst_ref=dst,
                send_sem=send_sem.at[phase, k, c],
                recv_sem=recv_sem.at[phase, k, c],
                device_id={"member": c, "space": sp},
                device_id_type=MESH,
            ).wait_recv()
        exchange(phase, k, 0).wait()

    def send(phase, k):
        for d in (2, 1, 3, 0):
            exchange(phase, k, d).start()

    def pack(source, tail):
        for c in range(MEMBERS):
            rows = tail_rows(c % 2)
            for j in range(4):
                pieces = []
                for s in range(4 * j, 4 * j + 4):
                    if s < len(rows):
                        pieces.append(source[rows[s], c // 2, :, TAIL:NY])
                    else:
                        pieces.append(jnp.zeros((OWN, NY - TAIL), F32))
                tail[c, j] = jnp.concatenate(pieces, axis=-1)

    for c in load_x:
        c.wait()
    for k in range(CHUNKS):
        send(0, k)
    pack(xv, xtail)
    send(0, CHUNKS)

    def halo(t, side):
        src = wave.at[t, pl.ds(GHOST if side == 0 else ROWS, GHOST)]
        dst = wave.at[t, pl.ds(GHOST + ROWS if side == 0 else 0, GHOST)]
        return pltpu.make_async_remote_copy(
            src_ref=src,
            dst_ref=dst,
            send_sem=hsend_sem.at[t, side],
            recv_sem=hrecv_sem.at[t, side],
            device_id={"member": me, "space": left if side == 0 else right},
            device_id_type=MESH,
        )

    def halo_start(t):
        @pl.when(has_left)
        def _():
            halo(t, 0).start()

        @pl.when(has_right)
        def _():
            halo(t, 1).start()

    def halo_wait(t):
        @pl.when(has_left)
        def _():
            halo(t, 1).wait_recv()

        @pl.when(has_right)
        def _():
            halo(t, 0).wait_recv()

    for c in load_n:
        c.wait()
    halo_start(0)

    for c in load_h:
        c.wait()

    @pl.loop(0, ROWS)
    def _(r):
        for z in range(2):
            total = jnp.zeros((OWN, NY), F32)
            for k in range(1, GHOST + 1):
                if k > z:
                    total = total + weights[k] * gh[r, GHOST - (k - z)]
                if k > 1 - z:
                    total = total + weights[k] * gh[r, GHOST - 1 + (k - (1 - z))]
            gz[r, z] = total
            coef[r, z] = jnp.square(courant * (1.0 + 0.3 * jnp.tanh(xv[r, z])))

    for c in load_p:
        c.wait()

    blank = jnp.zeros((OWN, WIDE - NY), F32)

    def row_step(t, r):
        amplitude = 2.0 * math.cos(1.3 * t)
        for z in range(2):
            center = wave[t, r + GHOST, z]
            wide = jnp.concatenate([center, blank], axis=-1)
            total = (3.0 * weights[0]) * center + gz[r, z] + weights[1] * wave[t, r + GHOST, 1 - z]
            for k in range(1, GHOST + 1):
                pair = wave[t, r + GHOST + k, z] + wave[t, r + GHOST - k, z]
                turned = pltpu.roll(wide, k, 1) + pltpu.roll(wide, WIDE - k, 1)
                total = total + weights[k] * (pair + turned[:, :NY])
            older = prev[r, z] if t == 0 else wave[t - 1, r + GHOST, z]
            following = 2.0 * center - older + coef[r, z] * total
            if z == 0:
                following = following + jnp.where(spot[...] == r, F32(amplitude), F32(0.0))
            if t == STEPS - 1:
                after[r, z] = following
            else:
                wave[t + 1, r + GHOST, z] = following
            if t == STEPS - 2:
                before[r, z] = following

    def edges(t):
        halo_wait(t)

        @pl.loop(0, 2 * GHOST)
        def _(i):
            row_step(t, jnp.where(i < GHOST, i, i + ROWS - 2 * GHOST))

        if t < STEPS - 1:
            halo_start(t + 1)

    def inner(t):
        @pl.loop(GHOST, ROWS - GHOST)
        def _(r):
            row_step(t, r)

    pairs = [(a, a, k) for a in range(MEMBERS) for k in range(1, 5)]
    pairs += [(a, b, k) for a in range(MEMBERS) for b in range(a + 1, MEMBERS) for k in range(8)]

    def add_pairs(load):
        blocks = [load(a) for a in range(MEMBERS)]
        turned = {}
        for n, (a, b, k) in enumerate(pairs):
            if (b, k) not in turned:
                turned[b, k] = blocks[b] if k == 0 else pltpu.roll(blocks[b], OWN - k, 0)
            gap = blocks[a] - turned[b, k]
            gap = gap * gap
            total = gap[:, :128]
            for i in range(1, gap.shape[1] // 128):
                total = total + gap[:, 128 * i : 128 * i + 128]
            acc[n] += total

    def distances(k):
        arrived(0, k)
        if k == CHUNKS:
            @pl.loop(0, 4)
            def _(j):
                add_pairs(lambda a: tails[j, OWN * a : OWN * a + OWN])
        else:
            @pl.loop(k * CHUNK, (k + 1) * CHUNK)
            def _(r):
                add_pairs(lambda a: cells[r, OWN * a : OWN * a + OWN])

    sub8 = lax.broadcasted_iota(jnp.int32, (OWN, 128), 0)
    lane8 = lax.broadcasted_iota(jnp.int32, (OWN, 128), 1)

    def matrix():
        m = jnp.zeros((OWN, 128), F32)
        for n, (a, b, k) in enumerate(pairs):
            v = jnp.broadcast_to(jnp.sum(acc[n], axis=1, keepdims=True), (OWN, 128))
            m = jnp.where(lane8 == COUNT * a + OWN * b + (sub8 + k) % OWN, v, m)
            if a != b or k < 4:
                v = v if k == 0 else pltpu.roll(v, k, 0)
                m = jnp.where(lane8 == COUNT * b + OWN * a + (sub8 + OWN - k) % OWN, v, m)
        return m

    def stage(n):
        if n == 0:
            return MEMBERS, me, lambda d: {"member": (me + d) % MEMBERS, "space": sp}, 0
        if n == 1:
            return 8, place, lambda d: {"member": me, "space": group * 8 + (place + d) % 8}, 4
        return 4, group, lambda d: {"member": me, "space": ((group + d) % 4) * 8 + place}, 12

    def share(n, d):
        size, mine, peer, base = stage(n)
        return pltpu.make_async_remote_copy(
            src_ref=part.at[base + mine],
            dst_ref=part.at[base + mine],
            send_sem=rsend_sem.at[base + d],
            recv_sem=rrecv_sem.at[base + mine],
            device_id=peer(d),
            device_id_type=MESH,
        )

    def reduce_start(n, value):
        size, mine, _, base = stage(n)
        part[base + mine] = value
        for d in range(1, size):
            share(n, d).start()

    def reduce_end(n):
        size, mine, peer, base = stage(n)
        for d in range(1, size):
            slot = base + (mine + d) % size
            pltpu.make_async_remote_copy(
                src_ref=part.at[slot],
                dst_ref=part.at[slot],
                send_sem=rsend_sem.at[base + d],
                recv_sem=rrecv_sem.at[slot],
                device_id=peer(d),
                device_id_type=MESH,
            ).wait_recv()
        total = part[base]
        for i in range(1, size):
            total = total + part[base + i]
        return total

    def mixing(dist):
        band = jnp.sum(dist, keepdims=True) / (COUNT * (COUNT - 1) * math.log(COUNT + 1))
        band = jnp.broadcast_to(band, (OWN, 128))
        kern = jnp.exp(-dist / band)
        for a in range(MEMBERS):
            mine = kern if a == 0 else pltpu.roll(kern, 128 - COUNT * a, 1)
            mine = jnp.where(lane8 < COUNT, mine, 0.0)
            total = jnp.sum(mine, axis=1, keepdims=True)
            on_x = jnp.where(lane8 == OWN * a + sub8, 1.0 + step_size * total, 0.0) - step_size * mine
            on_g = (0.5 * step_size) * band * mine
            both = on_x + pltpu.roll(on_g, COUNT, 1)
            high = both.astype(jnp.bfloat16).astype(F32)
            low = both - high
            kmat[OWN * a : OWN * a + OWN, :128] = high + pltpu.roll(high, 64, 1)
            kmat[OWN * a : OWN * a + OWN, 128:] = low + pltpu.roll(low, 64, 1)

    def mixed(data):
        high = data.astype(jnp.bfloat16)
        low = (data - high.astype(F32)).astype(jnp.bfloat16)
        stack = jnp.concatenate([high, low, high, low], axis=0)
        return jnp.dot(kmat[...].astype(jnp.bfloat16), stack, preferred_element_type=F32)

    def back(k, d):
        c = (me + d) % MEMBERS
        at = pl.ds(pl.multiple_of(c * OWN, 8), OWN)
        if k == CHUNKS:
            src = otail.at[:, at, :]
            dst = ntail.at[me]
        else:
            rows = pl.ds(k * CHUNK, CHUNK)
            src = out.at[rows, at, :]
            dst = new.at[rows, my_plane, :, pl.ds(my_lane, HALF)]
        if d == 0:
            return pltpu.make_async_copy(src, dst, own_sem.at[2, k])
        return pltpu.make_async_remote_copy(
            src_ref=src,
            dst_ref=dst,
            send_sem=send_sem.at[2, k, c],
            recv_sem=recv_sem.at[2, k, me],
            device_id={"member": c, "space": sp},
            device_id_type=MESH,
        )

    def back_arrived(k):
        for d in range(1, MEMBERS):
            c = (me + d) % MEMBERS
            if k == CHUNKS:
                dst = ntail.at[c]
            else:
                lanes = pl.ds(pl.multiple_of((c % 2) * HALF, 128), HALF)
                dst = new.at[pl.ds(k * CHUNK, CHUNK), c // 2, :, lanes]
            pltpu.make_async_remote_copy(
                src_ref=dst,
                dst_ref=dst,
                send_sem=send_sem.at[2, k, c],
                recv_sem=recv_sem.at[2, k, c],
                device_id={"member": c, "space": sp},
                device_id_type=MESH,
            ).wait_recv()
        back(k, 0).wait()

    def update(k):
        arrived(1, k)
        if k == CHUNKS:
            @pl.loop(0, 4)
            def _(j):
                otail[j] = mixed(tails[j])
        else:
            @pl.loop(k * CHUNK, (k + 1) * CHUNK)
            def _(r):
                out[r] = mixed(cells[r])
        for d in (2, 1, 3, 0):
            back(k, d).start()

    edges(0)
    inner(0)
    for c in load_g:
        c.wait()
    pack(gv, gtail)
    distances(0)
    send(1, CHUNKS)
    send(1, 0)
    edges(1)
    distances(1)
    send(1, 1)
    inner(1)
    distances(2)
    send(1, 2)
    distances(3)
    send(1, 3)
    distances(4)
    send(1, 4)
    distances(CHUNKS)
    reduce_start(0, matrix())
    edges(2)
    reduce_start(1, reduce_end(0))
    inner(2)
    reduce_start(2, reduce_end(1))
    edges(3)
    mixing(reduce_end(2))
    update(CHUNKS)
    for k in range(CHUNKS):
        update(k)
    inner(3)

    for k in range(CHUNKS + 1):
        for d in range(1, MEMBERS):
            exchange(0, k, d).wait_send()
            exchange(1, k, d).wait_send()
    back_arrived(CHUNKS)
    for k in range(CHUNKS):
        back_arrived(k)
    for c in range(MEMBERS):
        for s, r in enumerate(tail_rows(c % 2)):
            new[r, c // 2, :, TAIL:NY] = ntail[c, s // 4, :, 32 * (s % 4) : 32 * (s % 4) + 32]

    for k in range(CHUNKS + 1):
        for d in range(1, MEMBERS):
            back(k, d).wait_send()
    for t in range(STEPS):
        @pl.when(has_left)
        def _():
            halo(t, 0).wait_send()

        @pl.when(has_right)
        def _():
            halo(t, 1).wait_send()
    for n in range(3):
        for d in range(1, stage(n)[0]):
            share(n, d).wait_send()


def place_kernel(new, before, after, o_new, o_before, o_after, sem):
    copies = [
        pltpu.make_async_copy(src.at[:, :, p, :], dst.at[p], sem.at[n, p])
        for n, (src, dst) in enumerate(((new, o_new), (before, o_before), (after, o_after)))
        for p in range(OWN)
    ]
    for c in copies:
        c.start()
    for c in copies:
        c.wait()


def shards(particles, loglik_grad, wave_prev, wave_now, ghosts, src_cell):
    keep = lambda a: pltpu.with_memory_space_constraint(a, pltpu.HBM)
    turn = lambda a: a.transpose(0, 2, 1, 3)
    hbm = pl.BlockSpec(memory_space=pltpu.HBM)
    near = pl.BlockSpec(memory_space=pltpu.VMEM)
    vmem = lambda *s: pltpu.VMEM(s, F32)
    inside = jax.ShapeDtypeStruct((ROWS, 2, OWN, NY), F32)
    new, before, after = pl.pallas_call(
        kernel,
        out_shape=(inside,) * 3,
        in_specs=[hbm] * 6,
        out_specs=(near,) * 3,
        scratch_shapes=[
            pltpu.SMEM((OWN,), jnp.int32),
            vmem(ROWS, 2, OWN, NY),
            vmem(ROWS, 2, OWN, NY),
            vmem(ROWS, 2, OWN, NY),
            vmem(STEPS, ROWS + 2 * GHOST, 2, OWN, NY),
            vmem(ROWS, 2 * GHOST, OWN, NY),
            vmem(ROWS, 2, OWN, NY),
            vmem(ROWS, 2, OWN, NY),
            vmem(ROWS, 2 * COUNT, HALF),
            vmem(4, 2 * COUNT, 128),
            vmem(MEMBERS, 4, OWN, 128),
            vmem(MEMBERS, 4, OWN, 128),
            vmem(ROWS, COUNT, HALF),
            vmem(4, COUNT, 128),
            vmem(MEMBERS, 4, OWN, 128),
            pltpu.VMEM((OWN, NY), jnp.int32),
            vmem(64, OWN, 128),
            vmem(16, OWN, 128),
            vmem(COUNT, 256),
            pltpu.SemaphoreType.DMA((5, OWN)),
            pltpu.SemaphoreType.DMA,
            pltpu.SemaphoreType.DMA((3, CHUNKS + 1)),
            pltpu.SemaphoreType.DMA((3, CHUNKS + 1, MEMBERS)),
            pltpu.SemaphoreType.DMA((3, CHUNKS + 1, MEMBERS)),
            pltpu.SemaphoreType.DMA((STEPS, 2)),
            pltpu.SemaphoreType.DMA((STEPS, 2)),
            pltpu.SemaphoreType.DMA((16,)),
            pltpu.SemaphoreType.DMA((16,)),
        ],
        compiler_params=pltpu.CompilerParams(
            collective_id=0, has_side_effects=True, vmem_limit_bytes=48 * 1024 * 1024
        ),
    )(*map(keep, (turn(particles), turn(loglik_grad), turn(wave_prev), turn(wave_now), turn(ghosts), src_cell)))
    placed = jax.ShapeDtypeStruct((OWN, ROWS, 2, NY), F32)
    outs = pl.pallas_call(
        place_kernel,
        out_shape=(placed,) * 3,
        in_specs=[near] * 3,
        out_specs=(hbm,) * 3,
        scratch_shapes=[pltpu.SemaphoreType.DMA((3, OWN))],
        compiler_params=pltpu.CompilerParams(vmem_limit_bytes=4 * 1024 * 1024),
    )(new, before, after)
    return tuple(o.transpose(0, 2, 1, 3) for o in outs)


def solution(mesh):
    split = P("member", None, "space", None)
    return jax.shard_map(
        shards,
        mesh=mesh,
        in_specs=(split,) * 5 + (P("member"),),
        out_specs=(split,) * 3,
        check_vma=False,
    )
```

```python
import functools
import math

import jax
import jax.numpy as jnp
from jax import lax
from jax.experimental import pallas as pl
from jax.experimental.pallas import tpu as pltpu
from jax.sharding import PartitionSpec as P

MESH = pl.DeviceIdType.MESH
F32 = jnp.float32
GHOST = 4
STEPS = 4
MEMBERS = 4
OWN = 8
COUNT = 32
ROWS = 25
NY = 800
WIDE = 896
HALF = 384
TAIL = 768
CHUNKS = 5
CHUNK = ROWS // CHUNKS

weights = (-205.0 / 72.0, 8.0 / 5.0, -1.0 / 5.0, 8.0 / 315.0, -1.0 / 560.0)
step_size = 0.25
courant = 0.3


def tail_rows(half):
    return list(range(13)) if half == 0 else list(range(13, ROWS))


def kernel(
    x_hbm, g_hbm, wp_hbm, wn_hbm, gh_hbm, src_hbm,
    new, before, after,
    src_ref, xv, gv, prev, wave, gh, gz, coef,
    cells, tails, xtail, gtail, out, otail, ntail,
    spot, acc, part, kmat,
    load_sem, src_sem, own_sem, send_sem, recv_sem, hsend_sem, hrecv_sem, rsend_sem, rrecv_sem,
):
    me = lax.axis_index("member")
    sp = lax.axis_index("space")
    spaces = 32
    my_plane = me // 2
    my_lane = pl.multiple_of((me % 2) * HALF, 128)
    right = (sp + 1) % spaces
    left = (sp + spaces - 1) % spaces
    has_left = sp > 0
    has_right = sp < spaces - 1
    group = sp // 8
    place = sp % 8

    def loads(n, src, dst_of):
        return [
            pltpu.make_async_copy(src.at[p], dst_of(p), load_sem.at[n, p])
            for p in range(OWN)
        ]

    load_x = loads(0, x_hbm, lambda p: xv.at[:, :, p, :])
    load_n = loads(1, wn_hbm, lambda p: wave.at[0, pl.ds(GHOST, ROWS), :, p, :])
    load_h = loads(2, gh_hbm, lambda p: gh.at[:, :, p, :])
    load_p = loads(3, wp_hbm, lambda p: prev.at[:, :, p, :])
    load_g = loads(4, g_hbm, lambda p: gv.at[:, :, p, :])
    barrier = pltpu.get_barrier_semaphore()
    for d in range(1, MEMBERS):
        pl.semaphore_signal(
            barrier, inc=1, device_id={"member": (me + d) % MEMBERS, "space": sp}, device_id_type=MESH
        )
    peers = [group * 8 + (place + d) % 8 for d in range(1, 8)]
    peers += [((group + d) % 4) * 8 + place for d in range(1, 4)]
    peers += [left, right]
    for peer in peers:
        pl.semaphore_signal(barrier, inc=1, device_id={"member": me, "space": peer}, device_id_type=MESH)

    for c in load_x + load_n:
        c.start()
    pl.semaphore_wait(barrier, 15)

    def exchange(phase, k, d):
        c = (me + d) % MEMBERS
        source, tail = (xv, xtail) if phase == 0 else (gv, gtail)
        at = pl.ds(pl.multiple_of(phase * COUNT + me * OWN, 8), OWN)
        if k == CHUNKS:
            src = tail.at[c]
            dst = tails.at[:, at, :]
        else:
            rows = pl.ds(k * CHUNK, CHUNK)
            src = source.at[rows, c // 2, :, pl.ds(pl.multiple_of((c % 2) * HALF, 128), HALF)]
            dst = cells.at[rows, at, :]
        if d == 0:
            return pltpu.make_async_copy(src, dst, own_sem.at[phase, k])
        return pltpu.make_async_remote_copy(
            src_ref=src,
            dst_ref=dst,
            send_sem=send_sem.at[phase, k, c],
            recv_sem=recv_sem.at[phase, k, me],
            device_id={"member": c, "space": sp},
            device_id_type=MESH,
        )

    def arrived(phase, k):
        for d in range(1, MEMBERS):
            c = (me + d) % MEMBERS
            at = pl.ds(pl.multiple_of(phase * COUNT + c * OWN, 8), OWN)
            if k == CHUNKS:
                dst = tails.at[:, at, :]
            else:
                dst = cells.at[pl.ds(k * CHUNK, CHUNK), at, :]
            pltpu.make_async_remote_copy(
                src_ref=dst,
                dst_ref=dst,
                send_sem=send_sem.at[phase, k, c],
                recv_sem=recv_sem.at[phase, k, c],
                device_id={"member": c, "space": sp},
                device_id_type=MESH,
            ).wait_recv()
        exchange(phase, k, 0).wait()

    def send(phase, k):
        for d in (2, 1, 3, 0):
            exchange(phase, k, d).start()

    def pack(source, tail):
        for c in range(MEMBERS):
            rows = tail_rows(c % 2)
            for j in range(4):
                pieces = []
                for s in range(4 * j, 4 * j + 4):
                    if s < len(rows):
                        pieces.append(source[rows[s], c // 2, :, TAIL:NY])
                    else:
                        pieces.append(jnp.zeros((OWN, NY - TAIL), F32))
                tail[c, j] = jnp.concatenate(pieces, axis=-1)

    for c in load_x:
        c.wait()
    for k in range(CHUNKS):
        send(0, k)
    load_src = pltpu.make_async_copy(src_hbm, src_ref, src_sem)
    load_src.start()
    for c in load_h + load_p + load_g:
        c.start()
    pack(xv, xtail)
    send(0, CHUNKS)

    def halo(t, side):
        src = wave.at[t, pl.ds(GHOST if side == 0 else ROWS, GHOST)]
        dst = wave.at[t, pl.ds(GHOST + ROWS if side == 0 else 0, GHOST)]
        return pltpu.make_async_remote_copy(
            src_ref=src,
            dst_ref=dst,
            send_sem=hsend_sem.at[t, side],
            recv_sem=hrecv_sem.at[t, side],
            device_id={"member": me, "space": left if side == 0 else right},
            device_id_type=MESH,
        )

    def halo_start(t):
        @pl.when(has_left)
        def _():
            halo(t, 0).start()

        @pl.when(has_right)
        def _():
            halo(t, 1).start()

    def halo_wait(t):
        @pl.when(has_left)
        def _():
            halo(t, 1).wait_recv()

        @pl.when(has_right)
        def _():
            halo(t, 0).wait_recv()

    for c in load_n:
        c.wait()
    halo_start(0)

    acc[...] = jnp.zeros_like(acc)
    sub = lax.broadcasted_iota(jnp.int32, (OWN, NY), 0)
    lane = lax.broadcasted_iota(jnp.int32, (OWN, NY), 1)
    sx = jnp.full((OWN, NY), -1, jnp.int32)
    sy = jnp.full((OWN, NY), -1, jnp.int32)
    load_src.wait()
    for p in range(OWN):
        flat = src_ref[p]
        row = lax.div(flat, jnp.int32(NY))
        sx = jnp.where(sub == p, row - sp * ROWS, sx)
        sy = jnp.where(sub == p, flat - row * NY, sy)
    spot[...] = jnp.where(lane == sy, sx, -1)

    @pl.when(jnp.logical_not(has_left))
    def _():
        for t in range(STEPS):
            wave[t, 0:GHOST] = jnp.zeros((GHOST, 2, OWN, NY), F32)

    @pl.when(jnp.logical_not(has_right))
    def _():
        for t in range(STEPS):
            wave[t, GHOST + ROWS :] = jnp.zeros((GHOST, 2, OWN, NY), F32)

    for c in load_h:
        c.wait()

    @pl.loop(0, ROWS)
    def _(r):
        for z in range(2):
            total = jnp.zeros((OWN, NY), F32)
            for k in range(1, GHOST + 1):
                if k > z:
                    total = total + weights[k] * gh[r, GHOST - (k - z)]
                if k > 1 - z:
                    total = total + weights[k] * gh[r, GHOST - 1 + (k - (1 - z))]
            gz[r, z] = total
            coef[r, z] = jnp.square(courant * (1.0 + 0.3 * jnp.tanh(xv[r, z])))

    blank = jnp.zeros((OWN, WIDE - NY), F32)

    def row_step(t, r):
        amplitude = 2.0 * math.cos(1.3 * t)
        for z in range(2):
            center = wave[t, r + GHOST, z]
            wide = jnp.concatenate([center, blank], axis=-1)
            total = (3.0 * weights[0]) * center + gz[r, z] + weights[1] * wave[t, r + GHOST, 1 - z]
            for k in range(1, GHOST + 1):
                pair = wave[t, r + GHOST + k, z] + wave[t, r + GHOST - k, z]
                turned = pltpu.roll(wide, k, 1) + pltpu.roll(wide, WIDE - k, 1)
                total = total + weights[k] * (pair + turned[:, :NY])
            older = prev[r, z] if t == 0 else wave[t - 1, r + GHOST, z]
            following = 2.0 * center - older + coef[r, z] * total
            if z == 0:
                following = following + jnp.where(spot[...] == r, F32(amplitude), F32(0.0))
            if t == STEPS - 1:
                after[r, z] = following
            else:
                wave[t + 1, r + GHOST, z] = following
            if t == STEPS - 2:
                before[r, z] = following

    def edges(t):
        halo_wait(t)

        @pl.loop(0, 2 * GHOST)
        def _(i):
            row_step(t, jnp.where(i < GHOST, i, i + ROWS - 2 * GHOST))

        if t < STEPS - 1:
            halo_start(t + 1)

    def inner(t):
        @pl.loop(GHOST, ROWS - GHOST)
        def _(r):
            row_step(t, r)

    pairs = [(a, a, k) for a in range(MEMBERS) for k in range(1, 5)]
    pairs += [(a, b, k) for a in range(MEMBERS) for b in range(a + 1, MEMBERS) for k in range(8)]

    def add_pairs(load):
        blocks = [load(a) for a in range(MEMBERS)]
        turned = {}
        for n, (a, b, k) in enumerate(pairs):
            if (b, k) not in turned:
                turned[b, k] = blocks[b] if k == 0 else pltpu.roll(blocks[b], OWN - k, 0)
            gap = blocks[a] - turned[b, k]
            gap = gap * gap
            total = gap[:, :128]
            for i in range(1, gap.shape[1] // 128):
                total = total + gap[:, 128 * i : 128 * i + 128]
            acc[n] += total

    def distances(k):
        arrived(0, k)
        if k == CHUNKS:
            @pl.loop(0, 4)
            def _(j):
                add_pairs(lambda a: tails[j, OWN * a : OWN * a + OWN])
        else:
            @pl.loop(k * CHUNK, (k + 1) * CHUNK)
            def _(r):
                add_pairs(lambda a: cells[r, OWN * a : OWN * a + OWN])

    sub8 = lax.broadcasted_iota(jnp.int32, (OWN, 128), 0)
    lane8 = lax.broadcasted_iota(jnp.int32, (OWN, 128), 1)

    def matrix():
        m = jnp.zeros((OWN, 128), F32)
        for n, (a, b, k) in enumerate(pairs):
            v = jnp.broadcast_to(jnp.sum(acc[n], axis=1, keepdims=True), (OWN, 128))
            m = jnp.where(lane8 == COUNT * a + OWN * b + (sub8 + k) % OWN, v, m)
            if a != b or k < 4:
                v = v if k == 0 else pltpu.roll(v, k, 0)
                m = jnp.where(lane8 == COUNT * b + OWN * a + (sub8 + OWN - k) % OWN, v, m)
        return m

    def stage(n):
        if n == 0:
            return 8, place, lambda d: {"member": me, "space": group * 8 + (place + d) % 8}, 0
        if n == 1:
            return 4, group, lambda d: {"member": me, "space": ((group + d) % 4) * 8 + place}, 8
        return MEMBERS, me, lambda d: {"member": (me + d) % MEMBERS, "space": sp}, 12

    def share(n, d):
        size, mine, peer, base = stage(n)
        return pltpu.make_async_remote_copy(
            src_ref=part.at[base + mine],
            dst_ref=part.at[base + mine],
            send_sem=rsend_sem.at[base + d],
            recv_sem=rrecv_sem.at[base + mine],
            device_id=peer(d),
            device_id_type=MESH,
        )

    def reduce_start(n, value):
        size, mine, _, base = stage(n)
        part[base + mine] = value
        for d in range(1, size):
            share(n, d).start()

    def reduce_end(n):
        size, mine, peer, base = stage(n)
        for d in range(1, size):
            slot = base + (mine + d) % size
            pltpu.make_async_remote_copy(
                src_ref=part.at[slot],
                dst_ref=part.at[slot],
                send_sem=rsend_sem.at[base + d],
                recv_sem=rrecv_sem.at[slot],
                device_id=peer(d),
                device_id_type=MESH,
            ).wait_recv()
        total = part[base]
        for i in range(1, size):
            total = total + part[base + i]
        return total

    def mixing(dist):
        band = jnp.sum(dist, keepdims=True) / (COUNT * (COUNT - 1) * math.log(COUNT + 1))
        band = jnp.broadcast_to(band, (OWN, 128))
        kern = jnp.exp(-dist / band)
        for a in range(MEMBERS):
            mine = kern if a == 0 else pltpu.roll(kern, 128 - COUNT * a, 1)
            mine = jnp.where(lane8 < COUNT, mine, 0.0)
            total = jnp.sum(mine, axis=1, keepdims=True)
            on_x = jnp.where(lane8 == OWN * a + sub8, 1.0 + step_size * total, 0.0) - step_size * mine
            on_g = (0.5 * step_size) * band * mine
            both = on_x + pltpu.roll(on_g, COUNT, 1)
            high = both.astype(jnp.bfloat16).astype(F32)
            low = both - high
            kmat[OWN * a : OWN * a + OWN, :128] = high + pltpu.roll(high, 64, 1)
            kmat[OWN * a : OWN * a + OWN, 128:] = low + pltpu.roll(low, 64, 1)

    def mixed(data):
        high = data.astype(jnp.bfloat16)
        low = (data - high.astype(F32)).astype(jnp.bfloat16)
        stack = jnp.concatenate([high, low, high, low], axis=0)
        return jnp.dot(kmat[...].astype(jnp.bfloat16), stack, preferred_element_type=F32)

    def back(k, d):
        c = (me + d) % MEMBERS
        at = pl.ds(pl.multiple_of(c * OWN, 8), OWN)
        if k == CHUNKS:
            src = otail.at[:, at, :]
            dst = ntail.at[me]
        else:
            rows = pl.ds(k * CHUNK, CHUNK)
            src = out.at[rows, at, :]
            dst = new.at[rows, my_plane, :, pl.ds(my_lane, HALF)]
        if d == 0:
            return pltpu.make_async_copy(src, dst, own_sem.at[2, k])
        return pltpu.make_async_remote_copy(
            src_ref=src,
            dst_ref=dst,
            send_sem=send_sem.at[2, k, c],
            recv_sem=recv_sem.at[2, k, me],
            device_id={"member": c, "space": sp},
            device_id_type=MESH,
        )

    def back_arrived(k):
        for d in range(1, MEMBERS):
            c = (me + d) % MEMBERS
            if k == CHUNKS:
                dst = ntail.at[c]
            else:
                lanes = pl.ds(pl.multiple_of((c % 2) * HALF, 128), HALF)
                dst = new.at[pl.ds(k * CHUNK, CHUNK), c // 2, :, lanes]
            pltpu.make_async_remote_copy(
                src_ref=dst,
                dst_ref=dst,
                send_sem=send_sem.at[2, k, c],
                recv_sem=recv_sem.at[2, k, c],
                device_id={"member": c, "space": sp},
                device_id_type=MESH,
            ).wait_recv()
        back(k, 0).wait()

    def update(k):
        arrived(1, k)
        if k == CHUNKS:
            @pl.loop(0, 4)
            def _(j):
                otail[j] = mixed(tails[j])
        else:
            @pl.loop(k * CHUNK, (k + 1) * CHUNK)
            def _(r):
                out[r] = mixed(cells[r])
        for d in (2, 1, 3, 0):
            back(k, d).start()

    distances(0)
    for c in load_p:
        c.wait()
    edges(0)
    inner(0)
    for c in load_g:
        c.wait()
    pack(gv, gtail)
    send(1, CHUNKS)
    send(1, 0)
    send(1, 1)
    distances(1)
    distances(2)
    distances(3)
    distances(4)
    distances(CHUNKS)
    reduce_start(0, matrix())
    send(1, 2)
    edges(1)
    reduce_start(1, reduce_end(0))
    inner(1)
    reduce_start(2, reduce_end(1))
    send(1, 3)
    send(1, 4)
    edges(2)
    mixing(reduce_end(2))
    update(CHUNKS)
    update(0)
    update(1)
    update(2)
    inner(2)
    update(3)
    update(4)
    edges(3)
    inner(3)

    for k in range(CHUNKS + 1):
        for d in range(1, MEMBERS):
            exchange(0, k, d).wait_send()
            exchange(1, k, d).wait_send()
    back_arrived(CHUNKS)
    for c in range(MEMBERS):
        for s, r in enumerate(tail_rows(c % 2)):
            new[r, c // 2, :, TAIL:NY] = ntail[c, s // 4, :, 32 * (s % 4) : 32 * (s % 4) + 32]
    for k in range(CHUNKS):
        back_arrived(k)

    for k in range(CHUNKS + 1):
        for d in range(1, MEMBERS):
            back(k, d).wait_send()
    for t in range(STEPS):
        @pl.when(has_left)
        def _():
            halo(t, 0).wait_send()

        @pl.when(has_right)
        def _():
            halo(t, 1).wait_send()
    for n in range(3):
        for d in range(1, stage(n)[0]):
            share(n, d).wait_send()


def place_kernel(new, before, after, o_new, o_before, o_after, sem):
    copies = [
        pltpu.make_async_copy(src.at[:, :, p, :], dst.at[p], sem.at[n, p])
        for n, (src, dst) in enumerate(((new, o_new), (before, o_before), (after, o_after)))
        for p in range(OWN)
    ]
    for c in copies:
        c.start()
    for c in copies:
        c.wait()


def shards(particles, loglik_grad, wave_prev, wave_now, ghosts, src_cell):
    keep = lambda a: pltpu.with_memory_space_constraint(a, pltpu.HBM)
    turn = lambda a: a.transpose(0, 2, 1, 3)
    hbm = pl.BlockSpec(memory_space=pltpu.HBM)
    near = pl.BlockSpec(memory_space=pltpu.VMEM)
    vmem = lambda *s: pltpu.VMEM(s, F32)
    inside = jax.ShapeDtypeStruct((ROWS, 2, OWN, NY), F32)
    new, before, after = pl.pallas_call(
        kernel,
        out_shape=(inside,) * 3,
        in_specs=[hbm] * 6,
        out_specs=(near,) * 3,
        scratch_shapes=[
            pltpu.SMEM((OWN,), jnp.int32),
            vmem(ROWS, 2, OWN, NY),
            vmem(ROWS, 2, OWN, NY),
            vmem(ROWS, 2, OWN, NY),
            vmem(STEPS, ROWS + 2 * GHOST, 2, OWN, NY),
            vmem(ROWS, 2 * GHOST, OWN, NY),
            vmem(ROWS, 2, OWN, NY),
            vmem(ROWS, 2, OWN, NY),
            vmem(ROWS, 2 * COUNT, HALF),
            vmem(4, 2 * COUNT, 128),
            vmem(MEMBERS, 4, OWN, 128),
            vmem(MEMBERS, 4, OWN, 128),
            vmem(ROWS, COUNT, HALF),
            vmem(4, COUNT, 128),
            vmem(MEMBERS, 4, OWN, 128),
            pltpu.VMEM((OWN, NY), jnp.int32),
            vmem(64, OWN, 128),
            vmem(16, OWN, 128),
            vmem(COUNT, 256),
            pltpu.SemaphoreType.DMA((5, OWN)),
            pltpu.SemaphoreType.DMA,
            pltpu.SemaphoreType.DMA((3, CHUNKS + 1)),
            pltpu.SemaphoreType.DMA((3, CHUNKS + 1, MEMBERS)),
            pltpu.SemaphoreType.DMA((3, CHUNKS + 1, MEMBERS)),
            pltpu.SemaphoreType.DMA((STEPS, 2)),
            pltpu.SemaphoreType.DMA((STEPS, 2)),
            pltpu.SemaphoreType.DMA((16,)),
            pltpu.SemaphoreType.DMA((16,)),
        ],
        compiler_params=pltpu.CompilerParams(
            collective_id=0, has_side_effects=True, vmem_limit_bytes=48 * 1024 * 1024
        ),
    )(*map(keep, (turn(particles), turn(loglik_grad), turn(wave_prev), turn(wave_now), turn(ghosts), src_cell)))
    placed = jax.ShapeDtypeStruct((OWN, ROWS, 2, NY), F32)
    outs = pl.pallas_call(
        place_kernel,
        out_shape=(placed,) * 3,
        in_specs=[near] * 3,
        out_specs=(hbm,) * 3,
        scratch_shapes=[pltpu.SemaphoreType.DMA((3, OWN))],
        compiler_params=pltpu.CompilerParams(vmem_limit_bytes=4 * 1024 * 1024),
    )(new, before, after)
    return tuple(o.transpose(0, 2, 1, 3) for o in outs)


def solution(mesh):
    split = P("member", None, "space", None)
    return jax.shard_map(
        shards,
        mesh=mesh,
        in_specs=(split,) * 5 + (P("member"),),
        out_specs=(split,) * 3,
        check_vma=False,
    )
```

```python
import functools
import math

import jax
import jax.numpy as jnp
from jax import lax
from jax.experimental import pallas as pl
from jax.experimental.pallas import tpu as pltpu
from jax.sharding import PartitionSpec as P

MESH = pl.DeviceIdType.MESH
F32 = jnp.float32
GHOST = 4
STEPS = 4
MEMBERS = 4
OWN = 8
COUNT = 32
ROWS = 25
NY = 800
WIDE = 896
HALF = 384
TAIL = 768
CHUNKS = 5
CHUNK = ROWS // CHUNKS

weights = (-205.0 / 72.0, 8.0 / 5.0, -1.0 / 5.0, 8.0 / 315.0, -1.0 / 560.0)
step_size = 0.25
courant = 0.3


def tail_rows(half):
    return list(range(13)) if half == 0 else list(range(13, ROWS))


def kernel(
    x_hbm, g_hbm, wp_hbm, wn_hbm, gh_hbm, src_hbm,
    new, before, after,
    src_ref, xv, gv, prev, wave, gh, gz, coef,
    cells, tails, xtail, gtail, out, otail, ntail,
    spot, acc, part, kmat,
    load_sem, src_sem, own_sem, send_sem, recv_sem, hsend_sem, hrecv_sem, rsend_sem, rrecv_sem,
):
    me = lax.axis_index("member")
    sp = lax.axis_index("space")
    spaces = 32
    my_plane = me // 2
    my_lane = pl.multiple_of((me % 2) * HALF, 128)
    right = (sp + 1) % spaces
    left = (sp + spaces - 1) % spaces
    has_left = sp > 0
    has_right = sp < spaces - 1
    group = sp // 8
    place = sp % 8

    def loads(n, src, dst_of):
        return [
            pltpu.make_async_copy(src.at[p], dst_of(p), load_sem.at[n, p])
            for p in range(OWN)
        ]

    load_x = loads(0, x_hbm, lambda p: xv.at[:, :, p, :])
    load_n = loads(1, wn_hbm, lambda p: wave.at[0, pl.ds(GHOST, ROWS), :, p, :])
    load_h = loads(2, gh_hbm, lambda p: gh.at[:, :, p, :])
    load_p = loads(3, wp_hbm, lambda p: prev.at[:, :, p, :])
    load_g = loads(4, g_hbm, lambda p: gv.at[:, :, p, :])
    barrier = pltpu.get_barrier_semaphore()
    for d in range(1, MEMBERS):
        pl.semaphore_signal(
            barrier, inc=1, device_id={"member": (me + d) % MEMBERS, "space": sp}, device_id_type=MESH
        )
    peers = [group * 8 + (place + d) % 8 for d in range(1, 8)]
    peers += [((group + d) % 4) * 8 + place for d in range(1, 4)]
    peers += [left, right]
    for peer in peers:
        pl.semaphore_signal(barrier, inc=1, device_id={"member": me, "space": peer}, device_id_type=MESH)

    for c in load_x + load_n:
        c.start()
    pl.semaphore_wait(barrier, 15)

    def exchange(phase, k, d):
        c = (me + d) % MEMBERS
        source, tail = (xv, xtail) if phase == 0 else (gv, gtail)
        at = pl.ds(pl.multiple_of(phase * COUNT + me * OWN, 8), OWN)
        if k == CHUNKS:
            src = tail.at[c]
            dst = tails.at[:, at, :]
        else:
            rows = pl.ds(k * CHUNK, CHUNK)
            src = source.at[rows, c // 2, :, pl.ds(pl.multiple_of((c % 2) * HALF, 128), HALF)]
            dst = cells.at[rows, at, :]
        if d == 0:
            return pltpu.make_async_copy(src, dst, own_sem.at[phase, k])
        return pltpu.make_async_remote_copy(
            src_ref=src,
            dst_ref=dst,
            send_sem=send_sem.at[phase, k, c],
            recv_sem=recv_sem.at[phase, k, me],
            device_id={"member": c, "space": sp},
            device_id_type=MESH,
        )

    def arrived(phase, k):
        for d in range(1, MEMBERS):
            c = (me + d) % MEMBERS
            at = pl.ds(pl.multiple_of(phase * COUNT + c * OWN, 8), OWN)
            if k == CHUNKS:
                dst = tails.at[:, at, :]
            else:
                dst = cells.at[pl.ds(k * CHUNK, CHUNK), at, :]
            pltpu.make_async_remote_copy(
                src_ref=dst,
                dst_ref=dst,
                send_sem=send_sem.at[phase, k, c],
                recv_sem=recv_sem.at[phase, k, c],
                device_id={"member": c, "space": sp},
                device_id_type=MESH,
            ).wait_recv()
        exchange(phase, k, 0).wait()

    def send(phase, k):
        for d in (2, 1, 3, 0):
            exchange(phase, k, d).start()

    def pack(source, tail):
        for c in range(MEMBERS):
            rows = tail_rows(c % 2)
            for j in range(4):
                pieces = []
                for s in range(4 * j, 4 * j + 4):
                    if s < len(rows):
                        pieces.append(source[rows[s], c // 2, :, TAIL:NY])
                    else:
                        pieces.append(jnp.zeros((OWN, NY - TAIL), F32))
                tail[c, j] = jnp.concatenate(pieces, axis=-1)

    for c in load_x:
        c.wait()
    for k in range(CHUNKS):
        send(0, k)
    load_src = pltpu.make_async_copy(src_hbm, src_ref, src_sem)
    load_src.start()
    for c in load_h + load_p + load_g:
        c.start()
    pack(xv, xtail)
    send(0, CHUNKS)

    def halo(t, side):
        src = wave.at[t, pl.ds(GHOST if side == 0 else ROWS, GHOST)]
        dst = wave.at[t, pl.ds(GHOST + ROWS if side == 0 else 0, GHOST)]
        return pltpu.make_async_remote_copy(
            src_ref=src,
            dst_ref=dst,
            send_sem=hsend_sem.at[t, side],
            recv_sem=hrecv_sem.at[t, side],
            device_id={"member": me, "space": left if side == 0 else right},
            device_id_type=MESH,
        )

    def halo_start(t):
        @pl.when(has_left)
        def _():
            halo(t, 0).start()

        @pl.when(has_right)
        def _():
            halo(t, 1).start()

    def halo_wait(t):
        @pl.when(has_left)
        def _():
            halo(t, 1).wait_recv()

        @pl.when(has_right)
        def _():
            halo(t, 0).wait_recv()

    for c in load_n:
        c.wait()
    halo_start(0)

    acc[...] = jnp.zeros_like(acc)
    sub = lax.broadcasted_iota(jnp.int32, (OWN, NY), 0)
    lane = lax.broadcasted_iota(jnp.int32, (OWN, NY), 1)
    sx = jnp.full((OWN, NY), -1, jnp.int32)
    sy = jnp.full((OWN, NY), -1, jnp.int32)
    load_src.wait()
    for p in range(OWN):
        flat = src_ref[p]
        row = lax.div(flat, jnp.int32(NY))
        sx = jnp.where(sub == p, row - sp * ROWS, sx)
        sy = jnp.where(sub == p, flat - row * NY, sy)
    spot[...] = jnp.where(lane == sy, sx, -1)

    @pl.when(jnp.logical_not(has_left))
    def _():
        for t in range(STEPS):
            wave[t, 0:GHOST] = jnp.zeros((GHOST, 2, OWN, NY), F32)

    @pl.when(jnp.logical_not(has_right))
    def _():
        for t in range(STEPS):
            wave[t, GHOST + ROWS :] = jnp.zeros((GHOST, 2, OWN, NY), F32)

    for c in load_h:
        c.wait()

    @pl.loop(0, ROWS)
    def _(r):
        for z in range(2):
            total = jnp.zeros((OWN, NY), F32)
            for k in range(1, GHOST + 1):
                if k > z:
                    total = total + weights[k] * gh[r, GHOST - (k - z)]
                if k > 1 - z:
                    total = total + weights[k] * gh[r, GHOST - 1 + (k - (1 - z))]
            gz[r, z] = total
            coef[r, z] = jnp.square(courant * (1.0 + 0.3 * jnp.tanh(xv[r, z])))

    blank = jnp.zeros((OWN, WIDE - NY), F32)

    def row_step(t, r):
        amplitude = 2.0 * math.cos(1.3 * t)
        for z in range(2):
            center = wave[t, r + GHOST, z]
            wide = jnp.concatenate([center, blank], axis=-1)
            total = (3.0 * weights[0]) * center + gz[r, z] + weights[1] * wave[t, r + GHOST, 1 - z]
            for k in range(1, GHOST + 1):
                pair = wave[t, r + GHOST + k, z] + wave[t, r + GHOST - k, z]
                turned = pltpu.roll(wide, k, 1) + pltpu.roll(wide, WIDE - k, 1)
                total = total + weights[k] * (pair + turned[:, :NY])
            older = prev[r, z] if t == 0 else wave[t - 1, r + GHOST, z]
            following = 2.0 * center - older + coef[r, z] * total
            if z == 0:
                following = following + jnp.where(spot[...] == r, F32(amplitude), F32(0.0))
            if t == STEPS - 1:
                after[r, z] = following
            else:
                wave[t + 1, r + GHOST, z] = following
            if t == STEPS - 2:
                before[r, z] = following

    def edges(t):
        halo_wait(t)

        @pl.loop(0, 2 * GHOST)
        def _(i):
            row_step(t, jnp.where(i < GHOST, i, i + ROWS - 2 * GHOST))

        if t < STEPS - 1:
            halo_start(t + 1)

    def inner(t):
        @pl.loop(GHOST, ROWS - GHOST)
        def _(r):
            row_step(t, r)

    pairs = [(a, a, k) for a in range(MEMBERS) for k in range(1, 5)]
    pairs += [(a, b, k) for a in range(MEMBERS) for b in range(a + 1, MEMBERS) for k in range(8)]

    def add_pairs(load):
        blocks = [load(a) for a in range(MEMBERS)]
        turned = {}
        for n, (a, b, k) in enumerate(pairs):
            if (b, k) not in turned:
                turned[b, k] = blocks[b] if k == 0 else pltpu.roll(blocks[b], OWN - k, 0)
            gap = blocks[a] - turned[b, k]
            gap = gap * gap
            total = gap[:, :128]
            for i in range(1, gap.shape[1] // 128):
                total = total + gap[:, 128 * i : 128 * i + 128]
            acc[n] += total

    def distances(k):
        arrived(0, k)
        if k == CHUNKS:
            @pl.loop(0, 4)
            def _(j):
                add_pairs(lambda a: tails[j, OWN * a : OWN * a + OWN])
        else:
            @pl.loop(k * CHUNK, (k + 1) * CHUNK)
            def _(r):
                add_pairs(lambda a: cells[r, OWN * a : OWN * a + OWN])

    sub8 = lax.broadcasted_iota(jnp.int32, (OWN, 128), 0)
    lane8 = lax.broadcasted_iota(jnp.int32, (OWN, 128), 1)

    def matrix():
        m = jnp.zeros((OWN, 128), F32)
        for n, (a, b, k) in enumerate(pairs):
            v = jnp.broadcast_to(jnp.sum(acc[n], axis=1, keepdims=True), (OWN, 128))
            m = jnp.where(lane8 == COUNT * a + OWN * b + (sub8 + k) % OWN, v, m)
            if a != b or k < 4:
                v = v if k == 0 else pltpu.roll(v, k, 0)
                m = jnp.where(lane8 == COUNT * b + OWN * a + (sub8 + OWN - k) % OWN, v, m)
        return m

    def stage(n):
        if n == 0:
            return 8, place, lambda d: {"member": me, "space": group * 8 + (place + d) % 8}, 0
        if n == 1:
            return 4, group, lambda d: {"member": me, "space": ((group + d) % 4) * 8 + place}, 8
        return MEMBERS, me, lambda d: {"member": (me + d) % MEMBERS, "space": sp}, 12

    def share(n, d):
        size, mine, peer, base = stage(n)
        return pltpu.make_async_remote_copy(
            src_ref=part.at[base + mine],
            dst_ref=part.at[base + mine],
            send_sem=rsend_sem.at[base + d],
            recv_sem=rrecv_sem.at[base + mine],
            device_id=peer(d),
            device_id_type=MESH,
        )

    def reduce_start(n, value):
        size, mine, _, base = stage(n)
        part[base + mine] = value
        for d in range(1, size):
            share(n, d).start()

    def reduce_end(n):
        size, mine, peer, base = stage(n)
        for d in range(1, size):
            slot = base + (mine + d) % size
            pltpu.make_async_remote_copy(
                src_ref=part.at[slot],
                dst_ref=part.at[slot],
                send_sem=rsend_sem.at[base + d],
                recv_sem=rrecv_sem.at[slot],
                device_id=peer(d),
                device_id_type=MESH,
            ).wait_recv()
        total = part[base]
        for i in range(1, size):
            total = total + part[base + i]
        return total

    def mixing(dist):
        band = jnp.sum(dist, keepdims=True) / (COUNT * (COUNT - 1) * math.log(COUNT + 1))
        band = jnp.broadcast_to(band, (OWN, 128))
        kern = jnp.exp(-dist / band)
        for a in range(MEMBERS):
            mine = kern if a == 0 else pltpu.roll(kern, 128 - COUNT * a, 1)
            mine = jnp.where(lane8 < COUNT, mine, 0.0)
            total = jnp.sum(mine, axis=1, keepdims=True)
            on_x = jnp.where(lane8 == OWN * a + sub8, 1.0 + step_size * total, 0.0) - step_size * mine
            on_g = (0.5 * step_size) * band * mine
            both = on_x + pltpu.roll(on_g, COUNT, 1)
            high = both.astype(jnp.bfloat16).astype(F32)
            low = both - high
            kmat[OWN * a : OWN * a + OWN, :128] = high + pltpu.roll(high, 64, 1)
            kmat[OWN * a : OWN * a + OWN, 128:] = low + pltpu.roll(low, 64, 1)

    def mixed(data):
        high = data.astype(jnp.bfloat16)
        low = (data - high.astype(F32)).astype(jnp.bfloat16)
        stack = jnp.concatenate([high, low, high, low], axis=0)
        return jnp.dot(kmat[...].astype(jnp.bfloat16), stack, preferred_element_type=F32)

    def back(k, d):
        c = (me + d) % MEMBERS
        at = pl.ds(pl.multiple_of(c * OWN, 8), OWN)
        if k == CHUNKS:
            src = otail.at[:, at, :]
            dst = ntail.at[me]
        else:
            rows = pl.ds(k * CHUNK, CHUNK)
            src = out.at[rows, at, :]
            dst = new.at[rows, my_plane, :, pl.ds(my_lane, HALF)]
        if d == 0:
            return pltpu.make_async_copy(src, dst, own_sem.at[2, k])
        return pltpu.make_async_remote_copy(
            src_ref=src,
            dst_ref=dst,
            send_sem=send_sem.at[2, k, c],
            recv_sem=recv_sem.at[2, k, me],
            device_id={"member": c, "space": sp},
            device_id_type=MESH,
        )

    def back_arrived(k):
        for d in range(1, MEMBERS):
            c = (me + d) % MEMBERS
            if k == CHUNKS:
                dst = ntail.at[c]
            else:
                lanes = pl.ds(pl.multiple_of((c % 2) * HALF, 128), HALF)
                dst = new.at[pl.ds(k * CHUNK, CHUNK), c // 2, :, lanes]
            pltpu.make_async_remote_copy(
                src_ref=dst,
                dst_ref=dst,
                send_sem=send_sem.at[2, k, c],
                recv_sem=recv_sem.at[2, k, c],
                device_id={"member": c, "space": sp},
                device_id_type=MESH,
            ).wait_recv()
        back(k, 0).wait()

    def update(k):
        arrived(1, k)
        if k == CHUNKS:
            @pl.loop(0, 4)
            def _(j):
                otail[j] = mixed(tails[j])
        else:
            @pl.loop(k * CHUNK, (k + 1) * CHUNK)
            def _(r):
                out[r] = mixed(cells[r])
        for d in (2, 1, 3, 0):
            back(k, d).start()

    distances(0)
    for c in load_p:
        c.wait()
    edges(0)
    inner(0)
    for c in load_g:
        c.wait()
    pack(gv, gtail)
    distances(1)
    distances(2)
    edges(1)
    send(1, CHUNKS)
    send(1, 0)
    distances(3)
    distances(4)
    distances(CHUNKS)
    send(1, 1)
    reduce_start(0, matrix())
    send(1, 2)
    reduce_start(1, reduce_end(0))
    inner(1)
    reduce_start(2, reduce_end(1))
    send(1, 3)
    send(1, 4)
    edges(2)
    mixing(reduce_end(2))
    update(CHUNKS)
    update(0)
    update(1)
    update(2)
    inner(2)
    update(3)
    update(4)
    edges(3)
    inner(3)

    for k in range(CHUNKS + 1):
        for d in range(1, MEMBERS):
            exchange(0, k, d).wait_send()
            exchange(1, k, d).wait_send()
    back_arrived(CHUNKS)
    for c in range(MEMBERS):
        for s, r in enumerate(tail_rows(c % 2)):
            new[r, c // 2, :, TAIL:NY] = ntail[c, s // 4, :, 32 * (s % 4) : 32 * (s % 4) + 32]
    for k in range(CHUNKS):
        back_arrived(k)

    for k in range(CHUNKS + 1):
        for d in range(1, MEMBERS):
            back(k, d).wait_send()
    for t in range(STEPS):
        @pl.when(has_left)
        def _():
            halo(t, 0).wait_send()

        @pl.when(has_right)
        def _():
            halo(t, 1).wait_send()
    for n in range(3):
        for d in range(1, stage(n)[0]):
            share(n, d).wait_send()


def place_kernel(new, before, after, o_new, o_before, o_after, sem):
    copies = [
        pltpu.make_async_copy(src.at[:, :, p, :], dst.at[p], sem.at[n, p])
        for n, (src, dst) in enumerate(((new, o_new), (before, o_before), (after, o_after)))
        for p in range(OWN)
    ]
    for c in copies:
        c.start()
    for c in copies:
        c.wait()


def shards(particles, loglik_grad, wave_prev, wave_now, ghosts, src_cell):
    keep = lambda a: pltpu.with_memory_space_constraint(a, pltpu.HBM)
    turn = lambda a: a.transpose(0, 2, 1, 3)
    hbm = pl.BlockSpec(memory_space=pltpu.HBM)
    near = pl.BlockSpec(memory_space=pltpu.VMEM)
    vmem = lambda *s: pltpu.VMEM(s, F32)
    inside = jax.ShapeDtypeStruct((ROWS, 2, OWN, NY), F32)
    new, before, after = pl.pallas_call(
        kernel,
        out_shape=(inside,) * 3,
        in_specs=[hbm] * 6,
        out_specs=(near,) * 3,
        scratch_shapes=[
            pltpu.SMEM((OWN,), jnp.int32),
            vmem(ROWS, 2, OWN, NY),
            vmem(ROWS, 2, OWN, NY),
            vmem(ROWS, 2, OWN, NY),
            vmem(STEPS, ROWS + 2 * GHOST, 2, OWN, NY),
            vmem(ROWS, 2 * GHOST, OWN, NY),
            vmem(ROWS, 2, OWN, NY),
            vmem(ROWS, 2, OWN, NY),
            vmem(ROWS, 2 * COUNT, HALF),
            vmem(4, 2 * COUNT, 128),
            vmem(MEMBERS, 4, OWN, 128),
            vmem(MEMBERS, 4, OWN, 128),
            vmem(ROWS, COUNT, HALF),
            vmem(4, COUNT, 128),
            vmem(MEMBERS, 4, OWN, 128),
            pltpu.VMEM((OWN, NY), jnp.int32),
            vmem(64, OWN, 128),
            vmem(16, OWN, 128),
            vmem(COUNT, 256),
            pltpu.SemaphoreType.DMA((5, OWN)),
            pltpu.SemaphoreType.DMA,
            pltpu.SemaphoreType.DMA((3, CHUNKS + 1)),
            pltpu.SemaphoreType.DMA((3, CHUNKS + 1, MEMBERS)),
            pltpu.SemaphoreType.DMA((3, CHUNKS + 1, MEMBERS)),
            pltpu.SemaphoreType.DMA((STEPS, 2)),
            pltpu.SemaphoreType.DMA((STEPS, 2)),
            pltpu.SemaphoreType.DMA((16,)),
            pltpu.SemaphoreType.DMA((16,)),
        ],
        compiler_params=pltpu.CompilerParams(
            collective_id=0, has_side_effects=True, vmem_limit_bytes=48 * 1024 * 1024
        ),
    )(*map(keep, (turn(particles), turn(loglik_grad), turn(wave_prev), turn(wave_now), turn(ghosts), src_cell)))
    placed = jax.ShapeDtypeStruct((OWN, ROWS, 2, NY), F32)
    outs = pl.pallas_call(
        place_kernel,
        out_shape=(placed,) * 3,
        in_specs=[near] * 3,
        out_specs=(hbm,) * 3,
        scratch_shapes=[pltpu.SemaphoreType.DMA((3, OWN))],
        compiler_params=pltpu.CompilerParams(vmem_limit_bytes=4 * 1024 * 1024),
    )(new, before, after)
    return tuple(o.transpose(0, 2, 1, 3) for o in outs)


def solution(mesh):
    split = P("member", None, "space", None)
    return jax.shard_map(
        shards,
        mesh=mesh,
        in_specs=(split,) * 5 + (P("member"),),
        out_specs=(split,) * 3,
        check_vma=False,
    )
```

```python
import functools
import math

import jax
import jax.numpy as jnp
from jax import lax
from jax.experimental import pallas as pl
from jax.experimental.pallas import tpu as pltpu
from jax.sharding import PartitionSpec as P

MESH = pl.DeviceIdType.MESH
F32 = jnp.float32
GHOST = 4
STEPS = 4
MEMBERS = 4
OWN = 8
COUNT = 32
ROWS = 25
NY = 800
WIDE = 896
HALF = 384
TAIL = 768
CHUNKS = 5
CHUNK = ROWS // CHUNKS

weights = (-205.0 / 72.0, 8.0 / 5.0, -1.0 / 5.0, 8.0 / 315.0, -1.0 / 560.0)
step_size = 0.25
courant = 0.3


def tail_rows(half):
    return list(range(13)) if half == 0 else list(range(13, ROWS))


def kernel(
    x_hbm, g_hbm, wp_hbm, wn_hbm, gh_hbm, src_hbm,
    new, before, after,
    src_ref, xv, gv, prev, wave, gh, gz, coef,
    cells, tails, xtail, gtail, out, otail, ntail,
    spot, acc, part, kmat,
    load_sem, src_sem, own_sem, send_sem, recv_sem, hsend_sem, hrecv_sem, rsend_sem, rrecv_sem,
):
    me = lax.axis_index("member")
    sp = lax.axis_index("space")
    spaces = 32
    my_plane = me // 2
    my_lane = pl.multiple_of((me % 2) * HALF, 128)
    right = (sp + 1) % spaces
    left = (sp + spaces - 1) % spaces
    has_left = sp > 0
    has_right = sp < spaces - 1
    group = sp // 8
    place = sp % 8

    def loads(n, src, dst_of):
        return [
            pltpu.make_async_copy(src.at[p], dst_of(p), load_sem.at[n, p])
            for p in range(OWN)
        ]

    load_x = loads(0, x_hbm, lambda p: xv.at[:, :, p, :])
    load_n = loads(1, wn_hbm, lambda p: wave.at[0, pl.ds(GHOST, ROWS), :, p, :])
    load_h = loads(2, gh_hbm, lambda p: gh.at[:, :, p, :])
    load_p = loads(3, wp_hbm, lambda p: prev.at[:, :, p, :])
    load_g = loads(4, g_hbm, lambda p: gv.at[:, :, p, :])
    barrier = pltpu.get_barrier_semaphore()
    for d in range(1, MEMBERS):
        pl.semaphore_signal(
            barrier, inc=1, device_id={"member": (me + d) % MEMBERS, "space": sp}, device_id_type=MESH
        )
    peers = [group * 8 + (place + d) % 8 for d in range(1, 8)]
    peers += [((group + d) % 4) * 8 + place for d in range(1, 4)]
    peers += [left, right]
    for peer in peers:
        pl.semaphore_signal(barrier, inc=1, device_id={"member": me, "space": peer}, device_id_type=MESH)

    for c in load_x + load_n:
        c.start()
    pl.semaphore_wait(barrier, 15)

    def exchange(phase, k, d):
        c = (me + d) % MEMBERS
        source, tail = (xv, xtail) if phase == 0 else (gv, gtail)
        at = pl.ds(pl.multiple_of(phase * COUNT + me * OWN, 8), OWN)
        if k == CHUNKS:
            src = tail.at[c]
            dst = tails.at[:, at, :]
        else:
            rows = pl.ds(k * CHUNK, CHUNK)
            src = source.at[rows, c // 2, :, pl.ds(pl.multiple_of((c % 2) * HALF, 128), HALF)]
            dst = cells.at[rows, at, :]
        if d == 0:
            return pltpu.make_async_copy(src, dst, own_sem.at[phase, k])
        return pltpu.make_async_remote_copy(
            src_ref=src,
            dst_ref=dst,
            send_sem=send_sem.at[phase, k, c],
            recv_sem=recv_sem.at[phase, k, me],
            device_id={"member": c, "space": sp},
            device_id_type=MESH,
        )

    def arrived(phase, k):
        for d in range(1, MEMBERS):
            c = (me + d) % MEMBERS
            at = pl.ds(pl.multiple_of(phase * COUNT + c * OWN, 8), OWN)
            if k == CHUNKS:
                dst = tails.at[:, at, :]
            else:
                dst = cells.at[pl.ds(k * CHUNK, CHUNK), at, :]
            pltpu.make_async_remote_copy(
                src_ref=dst,
                dst_ref=dst,
                send_sem=send_sem.at[phase, k, c],
                recv_sem=recv_sem.at[phase, k, c],
                device_id={"member": c, "space": sp},
                device_id_type=MESH,
            ).wait_recv()
        exchange(phase, k, 0).wait()

    def send(phase, k):
        for d in (2, 1, 3, 0):
            exchange(phase, k, d).start()

    def pack(source, tail):
        for c in range(MEMBERS):
            rows = tail_rows(c % 2)
            for j in range(4):
                pieces = []
                for s in range(4 * j, 4 * j + 4):
                    if s < len(rows):
                        pieces.append(source[rows[s], c // 2, :, TAIL:NY])
                    else:
                        pieces.append(jnp.zeros((OWN, NY - TAIL), F32))
                tail[c, j] = jnp.concatenate(pieces, axis=-1)

    for c in load_x:
        c.wait()
    for k in range(CHUNKS):
        send(0, k)
    load_src = pltpu.make_async_copy(src_hbm, src_ref, src_sem)
    load_src.start()
    for c in load_h + load_p + load_g:
        c.start()
    pack(xv, xtail)
    send(0, CHUNKS)

    def halo(t, side):
        src = wave.at[t, pl.ds(GHOST if side == 0 else ROWS, GHOST)]
        dst = wave.at[t, pl.ds(GHOST + ROWS if side == 0 else 0, GHOST)]
        return pltpu.make_async_remote_copy(
            src_ref=src,
            dst_ref=dst,
            send_sem=hsend_sem.at[t, side],
            recv_sem=hrecv_sem.at[t, side],
            device_id={"member": me, "space": left if side == 0 else right},
            device_id_type=MESH,
        )

    def halo_start(t):
        @pl.when(has_left)
        def _():
            halo(t, 0).start()

        @pl.when(has_right)
        def _():
            halo(t, 1).start()

    def halo_wait(t):
        @pl.when(has_left)
        def _():
            halo(t, 1).wait_recv()

        @pl.when(has_right)
        def _():
            halo(t, 0).wait_recv()

    for c in load_n:
        c.wait()
    halo_start(0)

    acc[...] = jnp.zeros_like(acc)
    sub = lax.broadcasted_iota(jnp.int32, (OWN, NY), 0)
    lane = lax.broadcasted_iota(jnp.int32, (OWN, NY), 1)
    sx = jnp.full((OWN, NY), -1, jnp.int32)
    sy = jnp.full((OWN, NY), -1, jnp.int32)
    load_src.wait()
    for p in range(OWN):
        flat = src_ref[p]
        row = lax.div(flat, jnp.int32(NY))
        sx = jnp.where(sub == p, row - sp * ROWS, sx)
        sy = jnp.where(sub == p, flat - row * NY, sy)
    spot[...] = jnp.where(lane == sy, sx, -1)

    @pl.when(jnp.logical_not(has_left))
    def _():
        for t in range(STEPS):
            wave[t, 0:GHOST] = jnp.zeros((GHOST, 2, OWN, NY), F32)

    @pl.when(jnp.logical_not(has_right))
    def _():
        for t in range(STEPS):
            wave[t, GHOST + ROWS :] = jnp.zeros((GHOST, 2, OWN, NY), F32)

    for c in load_h:
        c.wait()

    @pl.loop(0, ROWS)
    def _(r):
        for z in range(2):
            total = jnp.zeros((OWN, NY), F32)
            for k in range(1, GHOST + 1):
                if k > z:
                    total = total + weights[k] * gh[r, GHOST - (k - z)]
                if k > 1 - z:
                    total = total + weights[k] * gh[r, GHOST - 1 + (k - (1 - z))]
            gz[r, z] = total
            coef[r, z] = jnp.square(courant * (1.0 + 0.3 * jnp.tanh(xv[r, z])))

    blank = jnp.zeros((OWN, WIDE - NY), F32)

    def row_step(t, r):
        amplitude = 2.0 * math.cos(1.3 * t)
        for z in range(2):
            center = wave[t, r + GHOST, z]
            wide = jnp.concatenate([center, blank], axis=-1)
            total = (3.0 * weights[0]) * center + gz[r, z] + weights[1] * wave[t, r + GHOST, 1 - z]
            for k in range(1, GHOST + 1):
                pair = wave[t, r + GHOST + k, z] + wave[t, r + GHOST - k, z]
                turned = pltpu.roll(wide, k, 1) + pltpu.roll(wide, WIDE - k, 1)
                total = total + weights[k] * (pair + turned[:, :NY])
            older = prev[r, z] if t == 0 else wave[t - 1, r + GHOST, z]
            following = 2.0 * center - older + coef[r, z] * total
            if z == 0:
                following = following + jnp.where(spot[...] == r, F32(amplitude), F32(0.0))
            if t == STEPS - 1:
                after[r, z] = following
            else:
                wave[t + 1, r + GHOST, z] = following
            if t == STEPS - 2:
                before[r, z] = following

    def edges(t):
        halo_wait(t)

        @pl.loop(0, 2 * GHOST)
        def _(i):
            row_step(t, jnp.where(i < GHOST, i, i + ROWS - 2 * GHOST))

        if t < STEPS - 1:
            halo_start(t + 1)

    def inner(t):
        @pl.loop(GHOST, ROWS - GHOST)
        def _(r):
            row_step(t, r)

    pairs = [(a, a, k) for a in range(MEMBERS) for k in range(1, 5)]
    pairs += [(a, b, k) for a in range(MEMBERS) for b in range(a + 1, MEMBERS) for k in range(8)]

    def add_pairs(load):
        blocks = [load(a) for a in range(MEMBERS)]
        turned = {}
        for n, (a, b, k) in enumerate(pairs):
            if (b, k) not in turned:
                turned[b, k] = blocks[b] if k == 0 else pltpu.roll(blocks[b], OWN - k, 0)
            gap = blocks[a] - turned[b, k]
            gap = gap * gap
            total = gap[:, :128]
            for i in range(1, gap.shape[1] // 128):
                total = total + gap[:, 128 * i : 128 * i + 128]
            acc[n] += total

    def distances(k):
        arrived(0, k)
        if k == CHUNKS:
            @pl.loop(0, 4)
            def _(j):
                add_pairs(lambda a: tails[j, OWN * a : OWN * a + OWN])
        else:
            @pl.loop(k * CHUNK, (k + 1) * CHUNK)
            def _(r):
                add_pairs(lambda a: cells[r, OWN * a : OWN * a + OWN])

    sub8 = lax.broadcasted_iota(jnp.int32, (OWN, 128), 0)
    lane8 = lax.broadcasted_iota(jnp.int32, (OWN, 128), 1)

    def matrix():
        m = jnp.zeros((OWN, 128), F32)
        for n, (a, b, k) in enumerate(pairs):
            v = jnp.broadcast_to(jnp.sum(acc[n], axis=1, keepdims=True), (OWN, 128))
            m = jnp.where(lane8 == COUNT * a + OWN * b + (sub8 + k) % OWN, v, m)
            if a != b or k < 4:
                v = v if k == 0 else pltpu.roll(v, k, 0)
                m = jnp.where(lane8 == COUNT * b + OWN * a + (sub8 + OWN - k) % OWN, v, m)
        return m

    def stage(n):
        if n == 0:
            return 8, place, lambda d: {"member": me, "space": group * 8 + (place + d) % 8}, 0
        if n == 1:
            return 4, group, lambda d: {"member": me, "space": ((group + d) % 4) * 8 + place}, 8
        return MEMBERS, me, lambda d: {"member": (me + d) % MEMBERS, "space": sp}, 12

    def share(n, d):
        size, mine, peer, base = stage(n)
        return pltpu.make_async_remote_copy(
            src_ref=part.at[base + mine],
            dst_ref=part.at[base + mine],
            send_sem=rsend_sem.at[base + d],
            recv_sem=rrecv_sem.at[base + mine],
            device_id=peer(d),
            device_id_type=MESH,
        )

    def reduce_start(n, value):
        size, mine, _, base = stage(n)
        part[base + mine] = value
        for d in range(1, size):
            share(n, d).start()

    def reduce_end(n):
        size, mine, peer, base = stage(n)
        for d in range(1, size):
            slot = base + (mine + d) % size
            pltpu.make_async_remote_copy(
                src_ref=part.at[slot],
                dst_ref=part.at[slot],
                send_sem=rsend_sem.at[base + d],
                recv_sem=rrecv_sem.at[slot],
                device_id=peer(d),
                device_id_type=MESH,
            ).wait_recv()
        total = part[base]
        for i in range(1, size):
            total = total + part[base + i]
        return total

    def mixing(dist):
        band = jnp.sum(dist, keepdims=True) / (COUNT * (COUNT - 1) * math.log(COUNT + 1))
        band = jnp.broadcast_to(band, (OWN, 128))
        kern = jnp.exp(-dist / band)
        for a in range(MEMBERS):
            mine = kern if a == 0 else pltpu.roll(kern, 128 - COUNT * a, 1)
            mine = jnp.where(lane8 < COUNT, mine, 0.0)
            total = jnp.sum(mine, axis=1, keepdims=True)
            on_x = jnp.where(lane8 == OWN * a + sub8, 1.0 + step_size * total, 0.0) - step_size * mine
            on_g = (0.5 * step_size) * band * mine
            both = on_x + pltpu.roll(on_g, COUNT, 1)
            high = both.astype(jnp.bfloat16).astype(F32)
            low = both - high
            kmat[OWN * a : OWN * a + OWN, :128] = high + pltpu.roll(high, 64, 1)
            kmat[OWN * a : OWN * a + OWN, 128:] = low + pltpu.roll(low, 64, 1)

    def mixed(data):
        high = data.astype(jnp.bfloat16)
        low = (data - high.astype(F32)).astype(jnp.bfloat16)
        stack = jnp.concatenate([high, low, high, low], axis=0)
        return jnp.dot(kmat[...].astype(jnp.bfloat16), stack, preferred_element_type=F32)

    def back(k, d):
        c = (me + d) % MEMBERS
        at = pl.ds(pl.multiple_of(c * OWN, 8), OWN)
        if k == CHUNKS:
            src = otail.at[:, at, :]
            dst = ntail.at[me]
        else:
            rows = pl.ds(k * CHUNK, CHUNK)
            src = out.at[rows, at, :]
            dst = new.at[rows, my_plane, :, pl.ds(my_lane, HALF)]
        if d == 0:
            return pltpu.make_async_copy(src, dst, own_sem.at[2, k])
        return pltpu.make_async_remote_copy(
            src_ref=src,
            dst_ref=dst,
            send_sem=send_sem.at[2, k, c],
            recv_sem=recv_sem.at[2, k, me],
            device_id={"member": c, "space": sp},
            device_id_type=MESH,
        )

    def back_arrived(k):
        for d in range(1, MEMBERS):
            c = (me + d) % MEMBERS
            if k == CHUNKS:
                dst = ntail.at[c]
            else:
                lanes = pl.ds(pl.multiple_of((c % 2) * HALF, 128), HALF)
                dst = new.at[pl.ds(k * CHUNK, CHUNK), c // 2, :, lanes]
            pltpu.make_async_remote_copy(
                src_ref=dst,
                dst_ref=dst,
                send_sem=send_sem.at[2, k, c],
                recv_sem=recv_sem.at[2, k, c],
                device_id={"member": c, "space": sp},
                device_id_type=MESH,
            ).wait_recv()
        back(k, 0).wait()

    def update(k):
        arrived(1, k)
        if k == CHUNKS:
            @pl.loop(0, 4)
            def _(j):
                otail[j] = mixed(tails[j])
        else:
            @pl.loop(k * CHUNK, (k + 1) * CHUNK)
            def _(r):
                out[r] = mixed(cells[r])
        for d in (2, 1, 3, 0):
            back(k, d).start()

    distances(0)
    for c in load_p:
        c.wait()
    edges(0)
    inner(0)
    for c in load_g:
        c.wait()
    pack(gv, gtail)
    distances(1)
    distances(2)
    edges(1)
    send(1, CHUNKS)
    send(1, 0)
    distances(3)
    distances(4)
    distances(CHUNKS)
    send(1, 1)
    reduce_start(0, matrix())
    send(1, 2)
    reduce_start(1, reduce_end(0))
    inner(1)
    reduce_start(2, reduce_end(1))
    send(1, 3)
    send(1, 4)
    mixing(reduce_end(2))
    update(CHUNKS)
    update(0)
    edges(2)
    update(1)
    update(2)
    inner(2)
    update(3)
    update(4)
    edges(3)
    inner(3)

    for k in range(CHUNKS + 1):
        for d in range(1, MEMBERS):
            exchange(0, k, d).wait_send()
            exchange(1, k, d).wait_send()
    back_arrived(CHUNKS)
    for c in range(MEMBERS):
        for s, r in enumerate(tail_rows(c % 2)):
            new[r, c // 2, :, TAIL:NY] = ntail[c, s // 4, :, 32 * (s % 4) : 32 * (s % 4) + 32]
    for k in range(CHUNKS):
        back_arrived(k)

    for k in range(CHUNKS + 1):
        for d in range(1, MEMBERS):
            back(k, d).wait_send()
    for t in range(STEPS):
        @pl.when(has_left)
        def _():
            halo(t, 0).wait_send()

        @pl.when(has_right)
        def _():
            halo(t, 1).wait_send()
    for n in range(3):
        for d in range(1, stage(n)[0]):
            share(n, d).wait_send()


def place_kernel(new, before, after, o_new, o_before, o_after, sem):
    copies = [
        pltpu.make_async_copy(src.at[:, :, p, :], dst.at[p], sem.at[n, p])
        for n, (src, dst) in enumerate(((new, o_new), (before, o_before), (after, o_after)))
        for p in range(OWN)
    ]
    for c in copies:
        c.start()
    for c in copies:
        c.wait()


def shards(particles, loglik_grad, wave_prev, wave_now, ghosts, src_cell):
    keep = lambda a: pltpu.with_memory_space_constraint(a, pltpu.HBM)
    turn = lambda a: a.transpose(0, 2, 1, 3)
    hbm = pl.BlockSpec(memory_space=pltpu.HBM)
    near = pl.BlockSpec(memory_space=pltpu.VMEM)
    vmem = lambda *s: pltpu.VMEM(s, F32)
    inside = jax.ShapeDtypeStruct((ROWS, 2, OWN, NY), F32)
    new, before, after = pl.pallas_call(
        kernel,
        out_shape=(inside,) * 3,
        in_specs=[hbm] * 6,
        out_specs=(near,) * 3,
        scratch_shapes=[
            pltpu.SMEM((OWN,), jnp.int32),
            vmem(ROWS, 2, OWN, NY),
            vmem(ROWS, 2, OWN, NY),
            vmem(ROWS, 2, OWN, NY),
            vmem(STEPS, ROWS + 2 * GHOST, 2, OWN, NY),
            vmem(ROWS, 2 * GHOST, OWN, NY),
            vmem(ROWS, 2, OWN, NY),
            vmem(ROWS, 2, OWN, NY),
            vmem(ROWS, 2 * COUNT, HALF),
            vmem(4, 2 * COUNT, 128),
            vmem(MEMBERS, 4, OWN, 128),
            vmem(MEMBERS, 4, OWN, 128),
            vmem(ROWS, COUNT, HALF),
            vmem(4, COUNT, 128),
            vmem(MEMBERS, 4, OWN, 128),
            pltpu.VMEM((OWN, NY), jnp.int32),
            vmem(64, OWN, 128),
            vmem(16, OWN, 128),
            vmem(COUNT, 256),
            pltpu.SemaphoreType.DMA((5, OWN)),
            pltpu.SemaphoreType.DMA,
            pltpu.SemaphoreType.DMA((3, CHUNKS + 1)),
            pltpu.SemaphoreType.DMA((3, CHUNKS + 1, MEMBERS)),
            pltpu.SemaphoreType.DMA((3, CHUNKS + 1, MEMBERS)),
            pltpu.SemaphoreType.DMA((STEPS, 2)),
            pltpu.SemaphoreType.DMA((STEPS, 2)),
            pltpu.SemaphoreType.DMA((16,)),
            pltpu.SemaphoreType.DMA((16,)),
        ],
        compiler_params=pltpu.CompilerParams(
            collective_id=0, has_side_effects=True, vmem_limit_bytes=48 * 1024 * 1024
        ),
    )(*map(keep, (turn(particles), turn(loglik_grad), turn(wave_prev), turn(wave_now), turn(ghosts), src_cell)))
    placed = jax.ShapeDtypeStruct((OWN, ROWS, 2, NY), F32)
    outs = pl.pallas_call(
        place_kernel,
        out_shape=(placed,) * 3,
        in_specs=[near] * 3,
        out_specs=(hbm,) * 3,
        scratch_shapes=[pltpu.SemaphoreType.DMA((3, OWN))],
        compiler_params=pltpu.CompilerParams(vmem_limit_bytes=4 * 1024 * 1024),
    )(new, before, after)
    return tuple(o.transpose(0, 2, 1, 3) for o in outs)


def solution(mesh):
    split = P("member", None, "space", None)
    return jax.shard_map(
        shards,
        mesh=mesh,
        in_specs=(split,) * 5 + (P("member"),),
        out_specs=(split,) * 3,
        check_vma=False,
    )
```
